32 devices in a mesh: groups: 2 (over y), wide: 4 (over x, core), narrow: 4 (over z).
Axes of the slice: x: 2, y: 2, z: 4, core: 2. Of those that a mesh axis runs over, the one named last changes fastest.
Arguments:
- features: bfloat16 [8192, 768], P(('groups', 'wide')), parts along dimension 0, may hold values from -6 to 6
- self_first: bfloat16 [768, 1024], P(None, 'narrow')
- neighbor_first: bfloat16 [768, 1024], P(None, 'narrow')
- self_second: bfloat16 [1024, 1024], P(None, 'narrow')
- neighbor_second: bfloat16 [1024, 1024], P(None, 'narrow')
- adjacency: bfloat16 [288, 128, 128], P(('groups', 'wide')), parts along dimension 0, may hold values from 0 to 1, as said below
- tile_rows: int32 [288], P(('groups', 'wide')), parts along dimension 0, may hold values from 0 to 7
- tile_cols: int32 [288], P(('groups', 'wide')), parts along dimension 0, may hold values from 0 to 23, as said below
- tile_count: int32 [8], P(('groups', 'wide')), parts along dimension 0, may hold values from 12 to 32, as said below
- send_blocks: int32 [32, 4], P(('groups', 'wide')), parts along dimension 0, may hold values from 0 to 7, as said below
Outputs:
- embeddings: bfloat16 [8192, 1024], P(('groups', 'wide'), 'narrow'), parts along dimension 0
The draws below stay inside these ranges and needn't reach their ends.
There are 2 independent parts, one for each index of `groups`. The reference program is written for one: setup_inputs(seed, part) draws one part's arguments, and reference() takes and returns one part's arrays. A program takes and returns all parts, laid end to end along the dimension named above; an argument that names none is the same for every part. Nothing has to cross between parts.
Inputs may be any that keep to these rules, and one draw needn't show every extreme that they name: `send_blocks`: in row p * 4 + q the entries are different blocks; the tiles of partition q read the first k of them, with k from 1 to 4 for p != q and 0 for p = q. `tile_cols`: live tiles read only slots that their sender fills. `tile_count`: each partition's live tiles stand first among its 36 slots. `adjacency`: entries are 0 or 1.
All inputs are finite; a program needn't handle non-finite values.
Results may differ from the reference program's by a relative error of at most 0.0065.
Values may be sent and summed in bfloat16 or wider, within the bound.
A program may use at most 128 MiB of HBM per device.

```python
import math
import jax
import jax.numpy as jnp
from jax import lax

F_IN = 768
F_HID = 1024
BLK = 128
B_DEV = 8
HALO_SLOTS = 4
EXTRA = 12
TMAX = 36
NODES = 4096
N_WIDE = 4


def structure(key):
    parts = N_WIDE
    slots = HALO_SLOTS
    keys = jax.random.split(key, 9)
    level = jax.random.randint(keys[0], (parts,), 0, 4)
    chosen = jax.random.randint(keys[1], (), 0, parts)
    is_chosen = jnp.arange(parts) == chosen
    level = jnp.where(is_chosen, 0, level)
    halving = jax.random.randint(keys[2], (parts, parts), 0, 2)
    halving = jnp.where(is_chosen[None, :], 0, halving)
    filled = jnp.maximum(jnp.right_shift(jnp.int32(slots), level[None, :] + halving), 1)
    diagonal = jnp.arange(parts)[:, None] == jnp.arange(parts)[None, :]
    filled = jnp.where(diagonal, 0, filled)
    scores = jax.random.randint(keys[3], (parts, parts, B_DEV), 0, 1 << 20) * B_DEV + jnp.arange(B_DEV, dtype=jnp.int32)
    sending = jnp.argsort(scores, axis=-1)[:, :, :slots].astype(jnp.int32)
    own_rows = jnp.broadcast_to(jnp.arange(B_DEV, dtype=jnp.int32), (parts, B_DEV))
    own_ok = jnp.ones((parts, B_DEV), jnp.int32)
    slot_index = jnp.arange(parts * slots, dtype=jnp.int32)
    halo_cols = jnp.broadcast_to(B_DEV + slot_index, (parts, parts * slots))
    halo_ok = ((slot_index % slots)[None, :] < filled.T[:, slot_index // slots]).astype(jnp.int32)
    halo_rows = jax.random.randint(keys[4], (parts, parts * slots), 0, B_DEV)
    extra_live = jnp.right_shift(jnp.int32(EXTRA), level)
    extra_ok = (jnp.arange(EXTRA, dtype=jnp.int32)[None, :] < extra_live[:, None]).astype(jnp.int32)
    extra_rows = jax.random.randint(keys[5], (parts, EXTRA), 0, B_DEV)
    sender = jax.random.randint(keys[6], (parts, EXTRA), 0, parts)
    receiver = jnp.broadcast_to(jnp.arange(parts, dtype=jnp.int32)[:, None], (parts, EXTRA))
    available = filled[sender, receiver]
    within = jax.random.randint(keys[7], (parts, EXTRA), 0, 1 << 20) % jnp.maximum(available, 1)
    local_pick = jax.random.randint(keys[8], (parts, EXTRA), 0, B_DEV)
    extra_cols = jnp.where(sender == receiver, local_pick, B_DEV + sender * slots + within)
    rows_all = jnp.concatenate([own_rows, halo_rows, extra_rows], axis=1)
    cols_all = jnp.concatenate([own_rows, halo_cols, extra_cols], axis=1)
    ok_all = jnp.concatenate([own_ok, halo_ok, extra_ok], axis=1)
    order = jnp.argsort(1 - ok_all, axis=1, stable=True)
    rows_sorted = jnp.take_along_axis(rows_all, order, axis=1).astype(jnp.int32)
    cols_sorted = jnp.take_along_axis(cols_all, order, axis=1).astype(jnp.int32)
    counts = jnp.sum(ok_all, axis=1).astype(jnp.int32)
    return (sending.reshape(parts * parts, slots), rows_sorted.reshape(-1), cols_sorted.reshape(-1), counts)


def column_scaled(values, key, spread, factor):
    fan_in = values.shape[0]
    columns = values.shape[1]
    position = jnp.arange(columns, dtype=jnp.float32) / columns
    jitter = jax.random.uniform(key, (columns,), jnp.float32)
    scales = jnp.power(3.0, position) * jnp.power(spread, jitter - 0.5)
    return (values * scales[None, :] * (factor / math.sqrt(fan_in))).astype(jnp.bfloat16)


def draw_send_blocks(key, part):
    return structure(key)[0]


def draw_tile_rows(key, part):
    return structure(key)[1]


def draw_tile_cols(key, part):
    return structure(key)[2]


def draw_tile_count(key, part):
    return structure(key)[3]


def draw_adjacency(key, part):
    shared = structure(key)
    key = jax.random.fold_in(key, 5)
    first, second, third = jax.random.split(key, 3)
    parts = N_WIDE
    threshold = jax.random.randint(first, (parts * TMAX, 1, 1), 2, 17)
    bits = jax.random.randint(second, (parts * TMAX, BLK, BLK), 0, BLK)
    alive = jax.random.randint(third, (parts, B_DEV, BLK), 0, 16) != 0
    owner_part = jnp.arange(parts * TMAX, dtype=jnp.int32) // TMAX
    alive_rows = alive[owner_part, shared[1]]
    edges = (bits < threshold) & alive_rows[:, :, None]
    return jnp.where(edges, 1.0, 0.0).astype(jnp.float32).astype(jnp.bfloat16)


def draw_self_first(key, part):
    key = jax.random.fold_in(key, 1)
    first, second = jax.random.split(key)
    values = jnp.clip(jax.random.normal(first, (F_IN, F_HID), jnp.float32), -6.0, 6.0)
    return column_scaled(values, second, 10.0, 1.0)


def draw_neighbor_first(key, part):
    key = jax.random.fold_in(key, 2)
    first, second = jax.random.split(key)
    values = jnp.clip(jax.random.normal(first, (F_IN, F_HID), jnp.float32), -6.0, 6.0)
    return column_scaled(values, second, 10.0, 3.0)


def draw_self_second(key, part):
    key = jax.random.fold_in(key, 3)
    first, second = jax.random.split(key)
    values = jnp.clip(jax.random.normal(first, (F_HID, F_HID), jnp.float32), -6.0, 6.0)
    return column_scaled(values, second, 10.0, 1.0)


def draw_neighbor_second(key, part):
    key = jax.random.fold_in(key, 4)
    first, second = jax.random.split(key)
    values = jnp.clip(jax.random.normal(first, (F_HID, F_HID), jnp.float32), -6.0, 6.0)
    return column_scaled(values, second, 10.0, 3.0)


def levels(rng, extent, cuts, least, top_value):
    level = 1.0
    for dim, blocks in cuts:
        draws = jax.random.uniform(jax.random.fold_in(jax.random.fold_in(rng, 6), dim), (blocks,), jnp.float32, least / len(cuts), top_value / len(cuts))
        level = level * jnp.repeat(jnp.exp(draws), extent[dim] // blocks).reshape((-1,) + (1,) * (len(extent) - 1 - dim))
    return level


def centred(stream_key, shape, deviation, bound, cuts=(), kind=jnp.bfloat16):
    entries = jax.random.normal(stream_key, shape, jnp.float32) * deviation
    if len(cuts) > 0:
        entries = levels(stream_key, shape, cuts, -0.22, 0.18) * entries
    return jnp.clip(entries, min=-bound, max=bound).astype(kind)


def setup_inputs(seed: int = 0, part: int = 0) -> dict:
    splits = jax.random.split(jax.random.key(seed), 11)
    part_keys = jax.random.split(jax.random.fold_in(splits[10], part), 11)
    return {
        "features": centred(part_keys[0], (NODES, F_IN), 1.0, 6.0, ((0, 4),)),
        "self_first": draw_self_first(jax.random.fold_in(splits[10], 71), part),
        "neighbor_first": draw_neighbor_first(jax.random.fold_in(splits[10], 71), part),
        "self_second": draw_self_second(jax.random.fold_in(splits[10], 71), part),
        "neighbor_second": draw_neighbor_second(jax.random.fold_in(splits[10], 71), part),
        "adjacency": draw_adjacency(jax.random.fold_in(jax.random.fold_in(splits[10], part), 71), part),
        "tile_rows": draw_tile_rows(jax.random.fold_in(jax.random.fold_in(splits[10], part), 71), part),
        "tile_cols": draw_tile_cols(jax.random.fold_in(jax.random.fold_in(splits[10], part), 71), part),
        "tile_count": draw_tile_count(jax.random.fold_in(jax.random.fold_in(splits[10], part), 71), part),
        "send_blocks": draw_send_blocks(jax.random.fold_in(jax.random.fold_in(splits[10], part), 71), part),
    }


def reference(features, self_first, neighbor_first, self_second, neighbor_second, adjacency, tile_rows, tile_cols, tile_count, send_blocks):
    highest = lax.Precision.HIGHEST
    partitions = N_WIDE
    tiles_by_part = adjacency.reshape(partitions, TMAX, BLK, BLK)
    rows_by_part = tile_rows.reshape(partitions, TMAX)
    cols_by_part = tile_cols.reshape(partitions, TMAX)
    sends = send_blocks.reshape(partitions, partitions, HALO_SLOTS)
    block_ids = jnp.arange(B_DEV, dtype=jnp.int32)
    positions = jnp.arange(TMAX, dtype=jnp.int32)

    def owners_of(part_index):
        usable = positions < tile_count[part_index]
        match = rows_by_part[part_index][None, :] == block_ids[:, None]
        return jnp.where(match & usable[None, :], 1.0, 0.0).astype(jnp.float32)

    def sources_of(part_index):
        columns = cols_by_part[part_index]
        slot = jnp.maximum(columns - B_DEV, 0).astype(jnp.int32)
        sender = (slot // HALO_SLOTS).astype(jnp.int32)
        within = (slot % HALO_SLOTS).astype(jnp.int32)
        remote = sender * B_DEV + sends[sender, part_index, within]
        local = part_index * B_DEV + columns
        return jnp.where(columns < B_DEV, local, remote).astype(jnp.int32)

    def neighbor_mean(projected):
        width = projected.shape[1]
        blocks = projected.reshape(partitions * B_DEV, BLK, width)

        def one_part(part_index):
            tiles_here = tiles_by_part[part_index].astype(jnp.float32)
            gathered = blocks[sources_of(part_index)]
            products = jnp.einsum('tij,tjf->tif', tiles_here, gathered, precision=highest)
            owners = owners_of(part_index)
            summed = jnp.einsum('bt,tif->bif', owners, products, precision=highest)
            degree = jnp.dot(owners, lax.optimization_barrier(jnp.sum(tiles_here, axis=2)), precision=highest)
            return summed / jnp.maximum(degree, 1.0)[:, :, None]
        averaged = lax.map(one_part, jnp.arange(partitions, dtype=jnp.int32))
        return averaged.reshape(partitions * B_DEV * BLK, width)

    def normalize(values, factor):
        summed = lax.optimization_barrier(jnp.sum(values * values, axis=1))
        return values * (lax.rsqrt(summed + 1e-06) * factor)[:, None]
    first_projected = jnp.dot(features, neighbor_first, preferred_element_type=jnp.float32)
    first_pre = jnp.dot(features, self_first, preferred_element_type=jnp.float32) + neighbor_mean(first_projected)
    hidden = normalize(jax.nn.relu(first_pre), 1.0).astype(jnp.bfloat16)
    second_projected = jnp.dot(hidden, neighbor_second, preferred_element_type=jnp.float32)
    second_pre = jnp.dot(hidden, self_second, preferred_element_type=jnp.float32) + neighbor_mean(second_projected)
    return normalize(second_pre, math.sqrt(F_HID)).astype(jnp.bfloat16)
```

```python
import functools
import math

import jax
import jax.numpy as jnp
from jax import lax
from jax.experimental import pallas as pl
from jax.experimental.pallas import tpu as pltpu
from jax.sharding import PartitionSpec as P

EPSILON = 1e-06
MESH = pl.DeviceIdType.MESH
F32 = jnp.float32
BF16 = jnp.bfloat16
VMEM_LIMIT = 56 * 1024 * 1024


def dot(a, b):
    return jnp.dot(a, b, preferred_element_type=F32)


def build_kernel(rows_ref, cols_ref, count_ref, adj_ref, a_ref, inv_ref):
    blk = adj_ref.shape[1]
    num_blocks = a_ref.shape[0] // blk
    ones = jnp.ones((blk, inv_ref.shape[1]), BF16)

    @pl.loop(0, num_blocks)
    def _(b):
        at = pl.ds(pl.multiple_of(b * blk, blk), blk)
        a_ref[at, :] = jnp.zeros((blk, a_ref.shape[1]), BF16)
        inv_ref[at, :] = jnp.zeros((blk, inv_ref.shape[1]), F32)

    @pl.loop(0, count_ref[0])
    def _(t):
        tile = adj_ref[t]
        rows = pl.ds(pl.multiple_of(rows_ref[t] * blk, blk), blk)
        cols = pl.ds(pl.multiple_of(cols_ref[t] * blk, blk), blk)
        a_ref[rows, cols] += tile
        inv_ref[rows, :] += dot(tile, ones)

    inv_ref[...] = 1.0 / jnp.maximum(inv_ref[...], 1.0)


def main_kernel(
    wide,
    narrow,
    step,
    factor,
    sb_ref,
    feat_ref,
    n1_ref,
    inv_ref,
    s1_hbm,
    s2_hbm,
    n2_hbm,
    a_hbm,
    out_ref,
    a,
    s1,
    s2,
    n2,
    own1,
    own2,
    halo1,
    halo2,
    out1,
    out2,
    pre,
    agg,
    hid,
    squares,
    part_sum,
    sums,
    load_sem,
    halo_send,
    halo_recv,
    right_send,
    left_send,
    hid_recv,
    sum_send,
    sum_recv,
):
    num_blocks, blk, cols = own1.shape
    nodes = num_blocks * blk
    slots = sb_ref.shape[1]
    depth = slots * blk
    chunks = nodes // step
    me = lax.axis_index("wide")
    n = lax.axis_index("narrow")

    loads = [
        pltpu.make_async_copy(src, dst, load_sem.at[i])
        for i, (src, dst) in enumerate([(s1_hbm, s1), (a_hbm, a), (n2_hbm, n2), (s2_hbm, s2)])
    ]
    for load in loads:
        load.start()

    barrier = pltpu.get_barrier_semaphore()
    for d in range(1, wide):
        pl.semaphore_signal(
            barrier, inc=1, device_id={"wide": lax.rem(me + d, wide)}, device_id_type=MESH
        )
    for d in range(1, narrow):
        pl.semaphore_signal(
            barrier, inc=1, device_id={"narrow": lax.rem(n + d, narrow)}, device_id_type=MESH
        )

    def rows_of(c):
        return pl.ds(pl.multiple_of(c * step, step), step)

    @pl.loop(0, num_blocks)
    def _(b):
        own1[b] = dot(feat_ref[pl.ds(pl.multiple_of(b * blk, blk), blk), :], n1_ref[...]).astype(BF16)

    pl.semaphore_wait(barrier, wide + narrow - 2)

    far = wide // 2
    order = [far] + [d for d in range(1, wide) if d != far]

    def halo_copy(layer, d):
        return pltpu.make_async_remote_copy(
            src_ref=(out1, out2)[layer].at[d - 1],
            dst_ref=(halo1, halo2)[layer].at[d - 1],
            send_sem=halo_send.at[layer, d - 1],
            recv_sem=halo_recv.at[layer, d - 1],
            device_id={"wide": lax.rem(me + d, wide)},
            device_id_type=MESH,
        )

    def send_halo(layer):
        own, out = ((own1, out1), (own2, out2))[layer]
        for d in order:
            q = lax.rem(me + d, wide)
            for s in range(slots):
                out[d - 1, s * blk : (s + 1) * blk, :] = own[sb_ref[q, s]]
            halo_copy(layer, d).start()

    def local_part(layer):
        own = (own1, own2)[layer]

        @pl.loop(0, chunks)
        def _(c):
            agg[rows_of(c), :] = dot(a[rows_of(c), 0:nodes], own[...].reshape(nodes, cols))

    def halo_term(layer, d, c):
        p = lax.rem(me + wide - d, wide)
        at = pl.ds(pl.multiple_of(nodes + p * depth, blk), depth)
        return dot(a[rows_of(c), at], (halo1, halo2)[layer][d - 1])

    def halo_part(layer):
        for d in order[:-1]:
            halo_copy(layer, d).wait_recv()

            @pl.loop(0, chunks)
            def _(c):
                agg[rows_of(c), :] += halo_term(layer, d, c)

        halo_copy(layer, order[-1]).wait_recv()

    def total(layer, c):
        mean = agg[rows_of(c), :] + halo_term(layer, order[-1], c)
        return pre[rows_of(c), 0:cols] + mean * inv_ref[rows_of(c), 0:1]

    def hid_copy(o, c, sems, target):
        return pltpu.make_async_remote_copy(
            src_ref=hid.at[o, rows_of(c)],
            dst_ref=hid.at[o, rows_of(c)],
            send_sem=sems.at[o, c],
            recv_sem=hid_recv.at[o, c],
            device_id={"narrow": target},
            device_id_type=MESH,
        )

    def to_right(o, c):
        return hid_copy(o, c, right_send, lax.rem(n + 1, narrow))

    def to_left(o, c):
        return hid_copy(o, c, left_send, lax.rem(n + narrow - 1, narrow))

    send_halo(0)
    loads[0].wait()

    @pl.loop(0, chunks)
    def _(c):
        pre[rows_of(c), 0:cols] = dot(feat_ref[rows_of(c), :], s1[...])

    loads[1].wait()
    local_part(0)
    halo_part(0)

    @pl.loop(0, chunks)
    def _(c):
        hid[n, rows_of(c)] = jnp.maximum(total(0, c), 0.0).astype(BF16)

        @pl.when(n < narrow - 1)
        def _():
            to_right(n, c).start()

        @pl.when(n > 0)
        def _():
            to_left(n, c).start()

    loads[2].wait()
    loads[3].wait()

    def consume(o, c, first=False):
        h = hid[o, rows_of(c)]
        at = pl.ds(pl.multiple_of(o * cols, cols), cols)
        wide_h = h.astype(F32)
        square = jnp.sum(wide_h * wide_h, axis=1, keepdims=True)
        self_term = dot(h, s2[at, :])
        neighbor_term = dot(h, n2[at, :])
        if first:
            squares[rows_of(c), :] = jnp.broadcast_to(square, (step, squares.shape[1]))
            pre[rows_of(c), 0:cols] = self_term
            agg[rows_of(c), :] = neighbor_term
        else:
            squares[rows_of(c), :] += square
            pre[rows_of(c), 0:cols] += self_term
            agg[rows_of(c), :] += neighbor_term

    @pl.loop(0, chunks)
    def _(c):
        consume(n, c, first=True)

    for dist in range(1, narrow):

        @pl.loop(0, chunks)
        def _(c):
            @pl.when(n >= dist)
            def _():
                to_right(n - dist, c).wait_recv()

                @pl.when(n < narrow - 1)
                def _():
                    to_right(n - dist, c).start()

            @pl.when(n + dist < narrow)
            def _():
                to_left(n + dist, c).wait_recv()

                @pl.when(n > 0)
                def _():
                    to_left(n + dist, c).start()

            @pl.when(n >= dist)
            def _():
                consume(n - dist, c)

            @pl.when(n + dist < narrow)
            def _():
                consume(n + dist, c)

    @pl.loop(0, chunks)
    def _(c):
        scale = lax.rsqrt(squares[rows_of(c), 0:1] + EPSILON)
        pre[rows_of(c), 0:cols] = pre[rows_of(c), 0:cols] * scale
        projected = (agg[rows_of(c), :] * scale).astype(BF16)
        per = step // blk
        own2[pl.ds(c * per, per)] = projected.reshape(per, blk, cols)

    send_halo(1)
    local_part(1)
    halo_part(1)

    ones = jnp.ones((part_sum.shape[0], cols), F32)

    @pl.loop(0, chunks)
    def _(c):
        value = total(1, c)
        pre[rows_of(c), 0:cols] = value
        part_sum[:, rows_of(c)] = lax.dot_general(
            ones,
            value * value,
            (((1,), (1,)), ((), ())),
            precision=lax.Precision.HIGHEST,
            preferred_element_type=F32,
        )

    def sum_copy(d):
        return pltpu.make_async_remote_copy(
            src_ref=part_sum,
            dst_ref=sums.at[d - 1],
            send_sem=sum_send.at[d - 1],
            recv_sem=sum_recv.at[d - 1],
            device_id={"narrow": lax.rem(n + d, narrow)},
            device_id_type=MESH,
        )

    for d in range(1, narrow):
        sum_copy(d).start()
    for d in range(1, narrow):
        sum_copy(d).wait_recv()

    @pl.loop(0, chunks)
    def _(c):
        summed = part_sum[:, rows_of(c)]
        for d in range(1, narrow):
            summed = summed + sums[d - 1, :, rows_of(c)]
        scale = lax.rsqrt(summed + EPSILON) * factor
        turned = jnp.broadcast_to(scale[0:1, :], (blk, step)).T
        out_ref[rows_of(c), :] = (pre[rows_of(c), 0:cols] * turned[:, 0:1]).astype(BF16)

    for d in range(1, narrow):
        sum_copy(d).wait_send()
    for layer in range(2):
        for d in order:
            halo_copy(layer, d).wait_send()

    for dist in range(narrow):

        @pl.loop(0, chunks)
        def _(c):
            @pl.when((n >= dist) & (n < narrow - 1))
            def _():
                to_right(n - dist, c).wait_send()

            @pl.when((n + dist < narrow) & (n > 0))
            def _():
                to_left(n + dist, c).wait_send()


def shards(
    wide,
    narrow,
    features,
    self_first,
    neighbor_first,
    self_second,
    neighbor_second,
    adjacency,
    tile_rows,
    tile_cols,
    tile_count,
    send_blocks,
):
    blk = adjacency.shape[1]
    nodes, in_width = features.shape
    num_blocks = nodes // blk
    slots = send_blocks.shape[1]
    hidden_width, cols = self_second.shape
    width = nodes + wide * slots * blk
    step = 2 * blk
    chunks = nodes // step
    vmem = pl.BlockSpec(memory_space=pltpu.VMEM)
    smem = pl.BlockSpec(memory_space=pltpu.SMEM)
    anywhere = pl.BlockSpec(memory_space=pl.ANY)
    matrix, inverse = pl.pallas_call(
        build_kernel,
        out_shape=(
            jax.ShapeDtypeStruct((nodes, width), BF16),
            jax.ShapeDtypeStruct((nodes, 128), F32),
        ),
        in_specs=[smem, smem, smem, vmem],
        out_specs=(vmem, vmem),
        compiler_params=pltpu.CompilerParams(vmem_limit_bytes=VMEM_LIMIT),
        name="build",
    )(tile_rows, tile_cols, tile_count, adjacency)
    dma = pltpu.SemaphoreType.DMA
    depth = slots * blk
    return pl.pallas_call(
        functools.partial(main_kernel, wide, narrow, step, math.sqrt(hidden_width)),
        out_shape=jax.ShapeDtypeStruct((nodes, cols), BF16),
        in_specs=[smem, vmem, vmem, vmem] + [anywhere] * 4,
        out_specs=vmem,
        scratch_shapes=[
            pltpu.VMEM((nodes, width), BF16),
            pltpu.VMEM((in_width, cols), BF16),
            pltpu.VMEM((hidden_width, cols), BF16),
            pltpu.VMEM((hidden_width, cols), BF16),
            pltpu.VMEM((num_blocks, blk, cols), BF16),
            pltpu.VMEM((num_blocks, blk, cols), BF16),
            pltpu.VMEM((wide - 1, depth, cols), BF16),
            pltpu.VMEM((wide - 1, depth, cols), BF16),
            pltpu.VMEM((wide - 1, depth, cols), BF16),
            pltpu.VMEM((wide - 1, depth, cols), BF16),
            pltpu.VMEM((nodes, cols), F32),
            pltpu.VMEM((nodes, cols), F32),
            pltpu.VMEM((narrow, nodes, cols), BF16),
            pltpu.VMEM((nodes, 128), F32),
            pltpu.VMEM((8, nodes), F32),
            pltpu.VMEM((narrow - 1, 8, nodes), F32),
            dma((4,)),
            dma((2, wide - 1)),
            dma((2, wide - 1)),
            dma((narrow, chunks)),
            dma((narrow, chunks)),
            dma((narrow, chunks)),
            dma((narrow - 1,)),
            dma((narrow - 1,)),
        ],
        compiler_params=pltpu.CompilerParams(
            collective_id=0, has_side_effects=True, vmem_limit_bytes=VMEM_LIMIT
        ),
        name="layers",
    )(
        send_blocks,
        features,
        neighbor_first,
        inverse,
        self_first,
        self_second,
        neighbor_second,
        matrix,
    )


def solution(mesh):
    in_specs = (
        P(("groups", "wide"), None),
        P(None, "narrow"),
        P(None, "narrow"),
        P(None, "narrow"),
        P(None, "narrow"),
        P(("groups", "wide"), None, None),
        P(("groups", "wide")),
        P(("groups", "wide")),
        P(("groups", "wide")),
        P(("groups", "wide"), None),
    )
    out_specs = P(("groups", "wide"), "narrow")
    body = functools.partial(shards, mesh.shape["wide"], mesh.shape["narrow"])
    return jax.shard_map(body, mesh=mesh, in_specs=in_specs, out_specs=out_specs, check_vma=False)
```

```python
import functools
import math

import jax
import jax.numpy as jnp
from jax import lax
from jax.experimental import pallas as pl
from jax.experimental.pallas import tpu as pltpu
from jax.sharding import PartitionSpec as P

EPSILON = 1e-06
MESH = pl.DeviceIdType.MESH
F32 = jnp.float32
BF16 = jnp.bfloat16
VMEM_LIMIT = 56 * 1024 * 1024


def dot(a, b):
    return jnp.dot(a, b, preferred_element_type=F32)


def index_kernel(num_blocks, rows_ref, cols_ref, count_ref, sb_ref, last_ref, prev_ref, out_ref):
    tiles = rows_ref.shape[0]
    width = last_ref.shape[0] // num_blocks
    partitions, slots = sb_ref.shape

    @pl.loop(0, last_ref.shape[0])
    def _(i):
        last_ref[i] = tiles

    @pl.loop(0, tiles)
    def _(t):
        prev_ref[t] = tiles

    @pl.loop(0, count_ref[0])
    def _(t):
        key = rows_ref[t] * width + cols_ref[t]
        prev_ref[t] = last_ref[key]
        last_ref[key] = t

    lane = lax.broadcasted_iota(jnp.int32, out_ref.shape[1:], 1)
    for q in range(partitions):
        value = jnp.zeros(out_ref.shape[1:], jnp.int32)
        for s in range(slots):
            value = jnp.where(lane == s, sb_ref[q, s], value)
        out_ref[q] = value


def main_kernel(
    wide,
    narrow,
    step,
    factor,
    sb_ref,
    last_ref,
    prev_ref,
    sbv_ref,
    feat_ref,
    n1_ref,
    s1_hbm,
    s2_hbm,
    n2_hbm,
    adj_hbm,
    out_ref,
    tiles,
    a,
    inv,
    s1,
    s2,
    n2,
    own1,
    halo1,
    out1,
    every,
    halo2,
    sbv_in,
    sb_in,
    pre,
    agg,
    hid,
    squares,
    part_sum,
    sums,
    load_sem,
    sb_send,
    sb_recv,
    halo_send,
    halo_recv,
    right_send,
    left_send,
    hid_recv,
    across_send,
    peer_send,
    every_recv,
    sum_send,
    sum_recv,
):
    num_blocks, blk, cols = own1.shape
    nodes = num_blocks * blk
    slots = sb_ref.shape[1]
    depth = slots * blk
    chunks = nodes // step
    per = step // blk
    pairs = wide // 2
    width = a.shape[1]
    num_tiles = prev_ref.shape[0]
    me = lax.axis_index("wide")
    n = lax.axis_index("narrow")
    pair = me // 2
    core = lax.rem(me, 2)
    other = 1 - core

    loads = [
        pltpu.make_async_copy(src, dst, load_sem.at[i])
        for i, (src, dst) in enumerate([(adj_hbm, tiles.at[pl.ds(0, num_tiles)]), (s1_hbm, s1), (n2_hbm, n2), (s2_hbm, s2)])
    ]
    for load in loads:
        load.start()

    barrier = pltpu.get_barrier_semaphore()
    for d in range(1, wide):
        pl.semaphore_signal(
            barrier, inc=1, device_id={"wide": lax.rem(me + d, wide)}, device_id_type=MESH
        )
    for d in range(1, narrow):
        pl.semaphore_signal(
            barrier, inc=1, device_id={"narrow": lax.rem(n + d, narrow)}, device_id_type=MESH
        )

    def rows_of(c):
        return pl.ds(pl.multiple_of(c * step, step), step)

    @pl.loop(0, num_blocks)
    def _(b):
        own1[b] = dot(feat_ref[pl.ds(pl.multiple_of(b * blk, blk), blk), :], n1_ref[...]).astype(BF16)

    pl.semaphore_wait(barrier, wide + narrow - 2)

    far = wide // 2
    order = [far] + [d for d in range(1, wide) if d != far]

    def sb_copy(q, p):
        return pltpu.make_async_remote_copy(
            src_ref=sbv_ref.at[q],
            dst_ref=sbv_in.at[p],
            send_sem=sb_send.at[q],
            recv_sem=sb_recv.at[p],
            device_id={"wide": q},
            device_id_type=MESH,
        )

    def halo_copy(d):
        return pltpu.make_async_remote_copy(
            src_ref=out1.at[d - 1],
            dst_ref=halo1.at[d - 1],
            send_sem=halo_send.at[d - 1],
            recv_sem=halo_recv.at[d - 1],
            device_id={"wide": lax.rem(me + d, wide)},
            device_id_type=MESH,
        )

    def halo_term(d, c):
        p = lax.rem(me + wide - d, wide)
        at = pl.ds(pl.multiple_of(nodes + p * depth, blk), depth)
        return dot(a[rows_of(c), at], halo1[d - 1])

    def hid_copy(o, c, sems, target):
        return pltpu.make_async_remote_copy(
            src_ref=hid.at[o, rows_of(c)],
            dst_ref=hid.at[o, rows_of(c)],
            send_sem=sems.at[o, c],
            recv_sem=hid_recv.at[o, c],
            device_id={"narrow": target},
            device_id_type=MESH,
        )

    def to_right(o, c):
        return hid_copy(o, c, right_send, lax.rem(n + 1, narrow))

    def to_left(o, c):
        return hid_copy(o, c, left_send, lax.rem(n + narrow - 1, narrow))

    def blocks_of(c):
        return pl.ds(c * per, per)

    def across_copy(dx, c):
        return pltpu.make_async_remote_copy(
            src_ref=every.at[0, core, blocks_of(c)],
            dst_ref=every.at[dx, core, blocks_of(c)],
            send_sem=across_send.at[dx - 1, c],
            recv_sem=every_recv.at[dx, core, c],
            device_id={"wide": lax.rem(pair + dx, pairs) * 2 + core},
            device_id_type=MESH,
        )

    def peer_copy(dx, side, c):
        return pltpu.make_async_remote_copy(
            src_ref=every.at[dx, side, blocks_of(c)],
            dst_ref=every.at[dx, side, blocks_of(c)],
            send_sem=peer_send.at[dx, c],
            recv_sem=every_recv.at[dx, side, c],
            device_id={"wide": pair * 2 + other},
            device_id_type=MESH,
        )

    def pass_on(c):
        for dx in range(1, pairs):
            across_copy(dx, c).wait_recv()
            peer_copy(dx, core, c).start()

    for d in order:
        q = lax.rem(me + d, wide)
        for s in range(slots):
            out1[d - 1, s * blk : (s + 1) * blk, :] = own1[sb_ref[q, s]]
        halo_copy(d).start()
    for d in order:
        sb_copy(lax.rem(me + d, wide), me).start()
    sbv_in[me] = sbv_ref[me]

    loads[0].wait()
    tiles[num_tiles] = jnp.zeros((blk, blk), BF16)

    @pl.loop(0, num_tiles)
    def _(t):
        tiles[t] += tiles[prev_ref[t]]

    @pl.loop(0, num_blocks)
    def _(b):
        for j in range(width // blk):
            at = pl.ds(pl.multiple_of(b * blk, blk), blk)
            a[at, j * blk : (j + 1) * blk] = tiles[last_ref[b * (width // blk) + j]]

    loads[1].wait()
    ones_tall = jnp.ones((width, blk), BF16)

    @pl.loop(0, chunks)
    def _(c):
        pre[rows_of(c), :] = dot(feat_ref[rows_of(c), :], s1[...])
        inv[rows_of(c), :] = 1.0 / jnp.maximum(dot(a[rows_of(c), :], ones_tall), 1.0)
        agg[rows_of(c), :] = dot(a[rows_of(c), 0:nodes], own1[...].reshape(nodes, cols))

    for d in order[1:] + order[:1]:
        halo_copy(d).wait_recv()
        if d != order[0]:

            @pl.loop(0, chunks)
            def _(c):
                agg[rows_of(c), :] += halo_term(d, c)

    @pl.loop(0, chunks)
    def _(c):
        mean = (agg[rows_of(c), :] + halo_term(order[0], c)) * inv[rows_of(c), 0:1]
        hid[n, rows_of(c)] = jnp.maximum(pre[rows_of(c), :] + mean, 0.0).astype(BF16)

        @pl.when(n < narrow - 1)
        def _():
            to_right(n, c).start()

        @pl.when(n > 0)
        def _():
            to_left(n, c).start()

    for d in order:
        sb_copy(me, lax.rem(me + d, wide)).wait_recv()
    to_scalar = pltpu.make_async_copy(sbv_in, sb_in, load_sem.at[4])
    to_scalar.start()
    to_scalar.wait()
    loads[2].wait()
    loads[3].wait()

    def consume(o, c, first=False):
        h = hid[o, rows_of(c)]
        at = pl.ds(pl.multiple_of(o * cols, cols), cols)
        wide_h = h.astype(F32)
        square = jnp.sum(wide_h * wide_h, axis=1, keepdims=True)
        self_term = dot(h, s2[at, :])
        neighbor_term = dot(h, n2[at, :])
        if first:
            squares[rows_of(c), :] = jnp.broadcast_to(square, (step, squares.shape[1]))
            pre[rows_of(c), :] = self_term
            agg[rows_of(c), :] = neighbor_term
        else:
            squares[rows_of(c), :] += square
            pre[rows_of(c), :] += self_term
            agg[rows_of(c), :] += neighbor_term

    @pl.loop(0, chunks)
    def _(c):
        consume(n, c, first=True)

    def finish(c):
        scale = lax.rsqrt(squares[rows_of(c), 0:1] + EPSILON)
        pre[rows_of(c), :] = pre[rows_of(c), :] * scale
        projected = (agg[rows_of(c), :] * scale).astype(BF16)
        every[0, core, blocks_of(c)] = projected.reshape(per, blk, cols)
        for dx in range(1, pairs):
            across_copy(dx, c).start()
        peer_copy(0, core, c).start()

    longest = jnp.maximum(n, narrow - 1 - n)

    @pl.loop(1, narrow)
    def _(dist):
        @pl.loop(0, chunks)
        def _(c):
            @pl.when(n >= dist)
            def _():
                to_right(n - dist, c).wait_recv()

                @pl.when(n < narrow - 1)
                def _():
                    to_right(n - dist, c).start()

            @pl.when(n + dist < narrow)
            def _():
                to_left(n + dist, c).wait_recv()

                @pl.when(n > 0)
                def _():
                    to_left(n + dist, c).start()

            @pl.when(n >= dist)
            def _():
                consume(n - dist, c)

            @pl.when(n + dist < narrow)
            def _():
                consume(n + dist, c)

            @pl.when(dist == longest)
            def _():
                finish(c)

                @pl.when(c > 0)
                def _():
                    pass_on(c - 1)

    @pl.loop(0, chunks)
    def _(c):
        agg[rows_of(c), :] = dot(a[rows_of(c), 0:nodes], every[0, core].reshape(nodes, cols))

    pass_on(chunks - 1)
    for dx in range(pairs):
        for c in range(chunks):
            peer_copy(dx, other, c).wait_recv()

    for p in range(wide):
        dx = lax.rem(pair + pairs - p // 2, pairs)
        for s in range(slots):
            at = p * depth + s * blk
            halo2[at : at + blk, :] = every[dx, p % 2, sb_in[p, 0, s]]

    ones = jnp.ones((part_sum.shape[0], cols), F32)

    @pl.loop(0, chunks)
    def _(c):
        total = agg[rows_of(c), :] + dot(a[rows_of(c), nodes:width], halo2[...])
        value = pre[rows_of(c), :] + total * inv[rows_of(c), 0:1]
        pre[rows_of(c), :] = value
        part_sum[:, rows_of(c)] = lax.dot_general(
            ones,
            value * value,
            (((1,), (1,)), ((), ())),
            precision=lax.Precision.HIGHEST,
            preferred_element_type=F32,
        )

    def sum_copy(d):
        return pltpu.make_async_remote_copy(
            src_ref=part_sum,
            dst_ref=sums.at[d - 1],
            send_sem=sum_send.at[d - 1],
            recv_sem=sum_recv.at[d - 1],
            device_id={"narrow": lax.rem(n + d, narrow)},
            device_id_type=MESH,
        )

    for d in range(1, narrow):
        sum_copy(d).start()
    for d in range(1, narrow):
        sum_copy(d).wait_recv()

    @pl.loop(0, chunks)
    def _(c):
        summed = part_sum[:, rows_of(c)]
        for d in range(1, narrow):
            summed = summed + sums[d - 1, :, rows_of(c)]
        scale = lax.rsqrt(summed + EPSILON) * factor
        turned = jnp.broadcast_to(scale[0:1, :], (blk, step)).T
        out_ref[rows_of(c), :] = (pre[rows_of(c), :] * turned[:, 0:1]).astype(BF16)

    for d in range(1, narrow):
        sum_copy(d).wait_send()
    for d in order:
        halo_copy(d).wait_send()
        sb_copy(lax.rem(me + d, wide), me).wait_send()

    @pl.loop(0, chunks)
    def _(c):
        for dx in range(1, pairs):
            across_copy(dx, c).wait_send()
            peer_copy(dx, core, c).wait_send()
        peer_copy(0, core, c).wait_send()

    @pl.loop(0, narrow)
    def _(dist):
        @pl.loop(0, chunks)
        def _(c):
            @pl.when((n >= dist) & (n < narrow - 1))
            def _():
                to_right(n - dist, c).wait_send()

            @pl.when((n + dist < narrow) & (n > 0))
            def _():
                to_left(n + dist, c).wait_send()


def shards(
    wide,
    narrow,
    features,
    self_first,
    neighbor_first,
    self_second,
    neighbor_second,
    adjacency,
    tile_rows,
    tile_cols,
    tile_count,
    send_blocks,
):
    blk = adjacency.shape[1]
    nodes, in_width = features.shape
    num_blocks = nodes // blk
    slots = send_blocks.shape[1]
    hidden_width, cols = self_second.shape
    width = nodes + wide * slots * blk
    step = 2 * blk
    chunks = nodes // step
    vmem = pl.BlockSpec(memory_space=pltpu.VMEM)
    smem = pl.BlockSpec(memory_space=pltpu.SMEM)
    anywhere = pl.BlockSpec(memory_space=pl.ANY)
    num_tiles = adjacency.shape[0]
    depth = slots * blk
    last, previous, index_rows = pl.pallas_call(
        functools.partial(index_kernel, num_blocks),
        out_shape=(
            jax.ShapeDtypeStruct((num_blocks * (width // blk),), jnp.int32),
            jax.ShapeDtypeStruct((num_tiles,), jnp.int32),
            jax.ShapeDtypeStruct((wide, 8, 128), jnp.int32),
        ),
        in_specs=[smem] * 4,
        out_specs=(smem, smem, vmem),
        name="index",
    )(tile_rows, tile_cols, tile_count, send_blocks)
    dma = pltpu.SemaphoreType.DMA
    return pl.pallas_call(
        functools.partial(main_kernel, wide, narrow, step, math.sqrt(hidden_width)),
        out_shape=jax.ShapeDtypeStruct((nodes, cols), BF16),
        in_specs=[smem] * 3 + [vmem] * 3 + [anywhere] * 4,
        out_specs=vmem,
        scratch_shapes=[
            pltpu.VMEM((num_tiles + 1, blk, blk), BF16),
            pltpu.VMEM((nodes, width), BF16),
            pltpu.VMEM((nodes, blk), F32),
            pltpu.VMEM((in_width, cols), BF16),
            pltpu.VMEM((hidden_width, cols), BF16),
            pltpu.VMEM((hidden_width, cols), BF16),
            pltpu.VMEM((num_blocks, blk, cols), BF16),
            pltpu.VMEM((wide - 1, depth, cols), BF16),
            pltpu.VMEM((wide - 1, depth, cols), BF16),
            pltpu.VMEM((wide // 2, 2, num_blocks, blk, cols), BF16),
            pltpu.VMEM((wide * depth, cols), BF16),
            pltpu.VMEM((wide, 8, 128), jnp.int32),
            pltpu.SMEM((wide, 8, 128), jnp.int32),
            pltpu.VMEM((nodes, cols), F32),
            pltpu.VMEM((nodes, cols), F32),
            pltpu.VMEM((narrow, nodes, cols), BF16),
            pltpu.VMEM((nodes, 128), F32),
            pltpu.VMEM((8, nodes), F32),
            pltpu.VMEM((narrow - 1, 8, nodes), F32),
            dma((5,)),
            dma((wide,)),
            dma((wide,)),
            dma((wide - 1,)),
            dma((wide - 1,)),
            dma((narrow, chunks)),
            dma((narrow, chunks)),
            dma((narrow, chunks)),
            dma((wide // 2 - 1, chunks)),
            dma((wide // 2, chunks)),
            dma((wide // 2, 2, chunks)),
            dma((narrow - 1,)),
            dma((narrow - 1,)),
        ],
        compiler_params=pltpu.CompilerParams(
            collective_id=0, has_side_effects=True, vmem_limit_bytes=VMEM_LIMIT
        ),
        name="layers",
    )(
        send_blocks,
        last,
        previous,
        index_rows,
        features,
        neighbor_first,
        self_first,
        self_second,
        neighbor_second,
        adjacency,
    )


def solution(mesh):
    in_specs = (
        P(("groups", "wide"), None),
        P(None, "narrow"),
        P(None, "narrow"),
        P(None, "narrow"),
        P(None, "narrow"),
        P(("groups", "wide"), None, None),
        P(("groups", "wide")),
        P(("groups", "wide")),
        P(("groups", "wide")),
        P(("groups", "wide"), None),
    )
    out_specs = P(("groups", "wide"), "narrow")
    body = functools.partial(shards, mesh.shape["wide"], mesh.shape["narrow"])
    return jax.shard_map(body, mesh=mesh, in_specs=in_specs, out_specs=out_specs, check_vma=False)
```

```python
import functools
import math

import jax
import jax.numpy as jnp
from jax import lax
from jax.experimental import pallas as pl
from jax.experimental.pallas import tpu as pltpu
from jax.sharding import PartitionSpec as P

EPSILON = 1e-06
MESH = pl.DeviceIdType.MESH
F32 = jnp.float32
BF16 = jnp.bfloat16
VMEM_LIMIT = 56 * 1024 * 1024


def dot(a, b):
    return jnp.dot(a, b, preferred_element_type=F32)


def main_kernel(
    wide,
    narrow,
    step,
    factor,
    sb_ref,
    rows_ref,
    cols_ref,
    count_ref,
    feat_hbm,
    n1_hbm,
    s1_hbm,
    s2_hbm,
    n2_hbm,
    adj_hbm,
    out_ref,
    feat_ref,
    n1_ref,
    tiles,
    a,
    inv,
    s1,
    s2,
    n2,
    own1,
    halo1,
    out1,
    every,
    halo2,
    table,
    table_in,
    sbv_ref,
    sbv_in,
    sb_in,
    pre,
    agg,
    hid,
    squares,
    part_sum,
    sums,
    load_sem,
    sb_send,
    sb_recv,
    halo_send,
    halo_recv,
    right_send,
    left_send,
    hid_recv,
    across_send,
    peer_send,
    every_recv,
    sum_send,
    sum_recv,
):
    num_blocks, blk, cols = own1.shape
    nodes = num_blocks * blk
    slots = sb_ref.shape[1]
    depth = slots * blk
    chunks = nodes // step
    per = step // blk
    pairs = wide // 2
    width = a.shape[1]
    num_tiles = rows_ref.shape[0]
    me = lax.axis_index("wide")
    n = lax.axis_index("narrow")
    pair = me // 2
    core = lax.rem(me, 2)
    other = 1 - core

    sources = [feat_hbm, n1_hbm, adj_hbm, s1_hbm, n2_hbm, s2_hbm]
    targets = [feat_ref, n1_ref, tiles.at[pl.ds(0, num_tiles)], s1, n2, s2]
    loads = [
        pltpu.make_async_copy(src, dst, load_sem.at[i])
        for i, (src, dst) in enumerate(zip(sources, targets))
    ]
    for load in loads:
        load.start()

    barrier = pltpu.get_barrier_semaphore()
    for d in range(1, wide):
        pl.semaphore_signal(
            barrier, inc=1, device_id={"wide": lax.rem(me + d, wide)}, device_id_type=MESH
        )
    for d in range(1, narrow):
        pl.semaphore_signal(
            barrier, inc=1, device_id={"narrow": lax.rem(n + d, narrow)}, device_id_type=MESH
        )

    lane = lax.broadcasted_iota(jnp.int32, (8, 128), 1)
    for q in range(wide):
        value = jnp.zeros((8, 128), jnp.int32)
        for s in range(slots):
            value = jnp.where(lane == s, sb_ref[q, s], value)
        sbv_ref[q] = value

    loads[0].wait()
    loads[1].wait()

    def rows_of(c):
        return pl.ds(pl.multiple_of(c * step, step), step)

    @pl.loop(0, num_blocks)
    def _(b):
        own1[b] = dot(feat_ref[pl.ds(pl.multiple_of(b * blk, blk), blk), :], n1_ref[...]).astype(BF16)

    pl.semaphore_wait(barrier, wide + narrow - 2)

    far = wide // 2
    order = [far] + [d for d in range(1, wide) if d != far]

    def sb_copy(q, p):
        return pltpu.make_async_remote_copy(
            src_ref=sbv_ref.at[q],
            dst_ref=sbv_in.at[p],
            send_sem=sb_send.at[q],
            recv_sem=sb_recv.at[p],
            device_id={"wide": q},
            device_id_type=MESH,
        )

    def halo_copy(d):
        return pltpu.make_async_remote_copy(
            src_ref=out1.at[d - 1],
            dst_ref=halo1.at[d - 1],
            send_sem=halo_send.at[d - 1],
            recv_sem=halo_recv.at[d - 1],
            device_id={"wide": lax.rem(me + d, wide)},
            device_id_type=MESH,
        )

    def halo_term(d, c):
        p = lax.rem(me + wide - d, wide)
        at = pl.ds(pl.multiple_of(nodes + p * depth, blk), depth)
        return dot(a[rows_of(c), at], halo1[d - 1])

    def hid_copy(o, c, sems, target):
        return pltpu.make_async_remote_copy(
            src_ref=hid.at[o, rows_of(c)],
            dst_ref=hid.at[o, rows_of(c)],
            send_sem=sems.at[o, c],
            recv_sem=hid_recv.at[o, c],
            device_id={"narrow": target},
            device_id_type=MESH,
        )

    def to_right(o, c):
        return hid_copy(o, c, right_send, lax.rem(n + 1, narrow))

    def to_left(o, c):
        return hid_copy(o, c, left_send, lax.rem(n + narrow - 1, narrow))

    def blocks_of(c):
        return pl.ds(c * per, per)

    def across_copy(dx, c):
        return pltpu.make_async_remote_copy(
            src_ref=every.at[0, core, blocks_of(c)],
            dst_ref=every.at[dx, core, blocks_of(c)],
            send_sem=across_send.at[dx - 1, c],
            recv_sem=every_recv.at[dx, core, c],
            device_id={"wide": lax.rem(pair + dx, pairs) * 2 + core},
            device_id_type=MESH,
        )

    def peer_copy(dx, side, c):
        return pltpu.make_async_remote_copy(
            src_ref=every.at[dx, side, blocks_of(c)],
            dst_ref=every.at[dx, side, blocks_of(c)],
            send_sem=peer_send.at[dx, c],
            recv_sem=every_recv.at[dx, side, c],
            device_id={"wide": pair * 2 + other},
            device_id_type=MESH,
        )

    def pass_on(c):
        for dx in range(1, pairs):
            across_copy(dx, c).wait_recv()
            peer_copy(dx, core, c).start()

    for d in order:
        q = lax.rem(me + d, wide)
        for s in range(slots):
            out1[d - 1, s * blk : (s + 1) * blk, :] = own1[sb_ref[q, s]]
        halo_copy(d).start()
    for d in order:
        sb_copy(lax.rem(me + d, wide), me).start()
    sbv_in[me] = sbv_ref[me]

    block_row = lax.broadcasted_iota(jnp.int32, (num_blocks, 128), 0)
    block_col = lax.broadcasted_iota(jnp.int32, (num_blocks, 128), 1)
    live = count_ref[0]

    def key_of(t):
        return jnp.where(t < live, rows_ref[t] * 128 + cols_ref[t], -1 - t)

    def gather_keys(t, keys):
        return jnp.where(lane == t, key_of(t), keys)

    keys = lax.fori_loop(0, num_tiles, gather_keys, jnp.full((8, 128), -1000, jnp.int32))

    def link(t, state):
        last, prev = state
        key = key_of(t)
        last = jnp.where(block_row * 128 + block_col == key, t, last)
        prev = jnp.where((keys == key) & (lane > t), t, prev)
        return last, prev

    empty = (
        jnp.full((num_blocks, 128), num_tiles, jnp.int32),
        jnp.full((8, 128), num_tiles, jnp.int32),
    )
    last, prev = lax.fori_loop(0, num_tiles, link, empty)
    table[0:num_blocks, :] = last
    table[num_blocks : num_blocks + 8, :] = prev
    to_scalar = pltpu.make_async_copy(table, table_in, load_sem.at[7])
    to_scalar.start()
    to_scalar.wait()

    loads[2].wait()
    tiles[num_tiles] = jnp.zeros((blk, blk), BF16)

    @pl.loop(0, num_tiles)
    def _(t):
        tiles[t] += tiles[table_in[num_blocks, t]]

    @pl.loop(0, num_blocks)
    def _(b):
        for j in range(width // blk):
            at = pl.ds(pl.multiple_of(b * blk, blk), blk)
            a[at, j * blk : (j + 1) * blk] = tiles[table_in[b, j]]

    loads[3].wait()
    ones_tall = jnp.ones((width, blk), BF16)

    @pl.loop(0, chunks)
    def _(c):
        pre[rows_of(c), :] = dot(feat_ref[rows_of(c), :], s1[...])
        inv[rows_of(c), :] = 1.0 / jnp.maximum(dot(a[rows_of(c), :], ones_tall), 1.0)
        agg[rows_of(c), :] = dot(a[rows_of(c), 0:nodes], own1[...].reshape(nodes, cols))

    for d in order[1:] + order[:1]:
        halo_copy(d).wait_recv()
        if d != order[0]:

            @pl.loop(0, chunks)
            def _(c):
                agg[rows_of(c), :] += halo_term(d, c)

    @pl.loop(0, chunks)
    def _(c):
        mean = (agg[rows_of(c), :] + halo_term(order[0], c)) * inv[rows_of(c), 0:1]
        hid[n, rows_of(c)] = jnp.maximum(pre[rows_of(c), :] + mean, 0.0).astype(BF16)

        @pl.when(n < narrow - 1)
        def _():
            to_right(n, c).start()

        @pl.when(n > 0)
        def _():
            to_left(n, c).start()

    for d in order:
        sb_copy(me, lax.rem(me + d, wide)).wait_recv()
    to_scalar = pltpu.make_async_copy(sbv_in, sb_in, load_sem.at[6])
    to_scalar.start()
    to_scalar.wait()
    loads[4].wait()
    loads[5].wait()

    def consume(o, c, first=False):
        h = hid[o, rows_of(c)]
        at = pl.ds(pl.multiple_of(o * cols, cols), cols)
        wide_h = h.astype(F32)
        square = jnp.sum(wide_h * wide_h, axis=1, keepdims=True)
        self_term = dot(h, s2[at, :])
        neighbor_term = dot(h, n2[at, :])
        if first:
            squares[rows_of(c), :] = jnp.broadcast_to(square, (step, squares.shape[1]))
            pre[rows_of(c), :] = self_term
            agg[rows_of(c), :] = neighbor_term
        else:
            squares[rows_of(c), :] += square
            pre[rows_of(c), :] += self_term
            agg[rows_of(c), :] += neighbor_term

    @pl.loop(0, chunks)
    def _(c):
        consume(n, c, first=True)

    def finish(c):
        scale = lax.rsqrt(squares[rows_of(c), 0:1] + EPSILON)
        pre[rows_of(c), :] = pre[rows_of(c), :] * scale
        projected = (agg[rows_of(c), :] * scale).astype(BF16)
        every[0, core, blocks_of(c)] = projected.reshape(per, blk, cols)
        for dx in range(1, pairs):
            across_copy(dx, c).start()
        peer_copy(0, core, c).start()

    longest = jnp.maximum(n, narrow - 1 - n)

    @pl.loop(1, narrow)
    def _(dist):
        @pl.loop(0, chunks)
        def _(c):
            @pl.when(n >= dist)
            def _():
                to_right(n - dist, c).wait_recv()

                @pl.when(n < narrow - 1)
                def _():
                    to_right(n - dist, c).start()

            @pl.when(n + dist < narrow)
            def _():
                to_left(n + dist, c).wait_recv()

                @pl.when(n > 0)
                def _():
                    to_left(n + dist, c).start()

            @pl.when(n >= dist)
            def _():
                consume(n - dist, c)

            @pl.when(n + dist < narrow)
            def _():
                consume(n + dist, c)

            @pl.when(dist == longest)
            def _():
                finish(c)

                @pl.when(c > 0)
                def _():
                    pass_on(c - 1)

    @pl.loop(0, chunks)
    def _(c):
        agg[rows_of(c), :] = dot(a[rows_of(c), 0:nodes], every[0, core].reshape(nodes, cols))

    pass_on(chunks - 1)
    for dx in range(pairs):
        for c in range(chunks):
            peer_copy(dx, other, c).wait_recv()

    for p in range(wide):
        dx = lax.rem(pair + pairs - p // 2, pairs)
        for s in range(slots):
            at = p * depth + s * blk
            halo2[at : at + blk, :] = every[dx, p % 2, sb_in[p, 0, s]]

    @pl.loop(0, chunks)
    def _(c):
        total = agg[rows_of(c), :] + dot(a[rows_of(c), nodes:width], halo2[...])
        value = pre[rows_of(c), :] + total * inv[rows_of(c), 0:1]
        pre[rows_of(c), :] = value
        row_sum = jnp.sum(value * value, axis=1, keepdims=True)
        part_sum[:, rows_of(c)] = jnp.broadcast_to(row_sum, (step, blk)).T[0:8, :]

    def sum_copy(d):
        return pltpu.make_async_remote_copy(
            src_ref=part_sum,
            dst_ref=sums.at[d - 1],
            send_sem=sum_send.at[d - 1],
            recv_sem=sum_recv.at[d - 1],
            device_id={"narrow": lax.rem(n + d, narrow)},
            device_id_type=MESH,
        )

    for d in range(1, narrow):
        sum_copy(d).start()
    for d in range(1, narrow):
        sum_copy(d).wait_recv()

    @pl.loop(0, chunks)
    def _(c):
        summed = part_sum[:, rows_of(c)]
        for d in range(1, narrow):
            summed = summed + sums[d - 1, :, rows_of(c)]
        scale = lax.rsqrt(summed + EPSILON) * factor
        turned = jnp.broadcast_to(scale[0:1, :], (blk, step)).T
        out_ref[rows_of(c), :] = (pre[rows_of(c), :] * turned[:, 0:1]).astype(BF16)

    for d in range(1, narrow):
        sum_copy(d).wait_send()
    for d in order:
        halo_copy(d).wait_send()
        sb_copy(lax.rem(me + d, wide), me).wait_send()

    @pl.loop(0, chunks)
    def _(c):
        for dx in range(1, pairs):
            across_copy(dx, c).wait_send()
            peer_copy(dx, core, c).wait_send()
        peer_copy(0, core, c).wait_send()

    @pl.loop(0, narrow)
    def _(dist):
        @pl.loop(0, chunks)
        def _(c):
            @pl.when((n >= dist) & (n < narrow - 1))
            def _():
                to_right(n - dist, c).wait_send()

            @pl.when((n + dist < narrow) & (n > 0))
            def _():
                to_left(n + dist, c).wait_send()


def shards(
    wide,
    narrow,
    features,
    self_first,
    neighbor_first,
    self_second,
    neighbor_second,
    adjacency,
    tile_rows,
    tile_cols,
    tile_count,
    send_blocks,
):
    blk = adjacency.shape[1]
    nodes, in_width = features.shape
    num_blocks = nodes // blk
    slots = send_blocks.shape[1]
    hidden_width, cols = self_second.shape
    width = nodes + wide * slots * blk
    step = 2 * blk
    chunks = nodes // step
    vmem = pl.BlockSpec(memory_space=pltpu.VMEM)
    smem = pl.BlockSpec(memory_space=pltpu.SMEM)
    anywhere = pl.BlockSpec(memory_space=pl.ANY)
    num_tiles = adjacency.shape[0]
    depth = slots * blk
    dma = pltpu.SemaphoreType.DMA
    return pl.pallas_call(
        functools.partial(main_kernel, wide, narrow, step, math.sqrt(hidden_width)),
        out_shape=jax.ShapeDtypeStruct((nodes, cols), BF16),
        in_specs=[smem] * 4 + [anywhere] * 6,
        out_specs=vmem,
        scratch_shapes=[
            pltpu.VMEM((nodes, in_width), BF16),
            pltpu.VMEM((in_width, cols), BF16),
            pltpu.VMEM((num_tiles + 1, blk, blk), BF16),
            pltpu.VMEM((nodes, width), BF16),
            pltpu.VMEM((nodes, blk), F32),
            pltpu.VMEM((in_width, cols), BF16),
            pltpu.VMEM((hidden_width, cols), BF16),
            pltpu.VMEM((hidden_width, cols), BF16),
            pltpu.VMEM((num_blocks, blk, cols), BF16),
            pltpu.VMEM((wide - 1, depth, cols), BF16),
            pltpu.VMEM((wide - 1, depth, cols), BF16),
            pltpu.VMEM((wide // 2, 2, num_blocks, blk, cols), BF16),
            pltpu.VMEM((wide * depth, cols), BF16),
            pltpu.VMEM((num_blocks + 8, 128), jnp.int32),
            pltpu.SMEM((num_blocks + 8, 128), jnp.int32),
            pltpu.VMEM((wide, 8, 128), jnp.int32),
            pltpu.VMEM((wide, 8, 128), jnp.int32),
            pltpu.SMEM((wide, 8, 128), jnp.int32),
            pltpu.VMEM((nodes, cols), F32),
            pltpu.VMEM((nodes, cols), F32),
            pltpu.VMEM((narrow, nodes, cols), BF16),
            pltpu.VMEM((nodes, 128), F32),
            pltpu.VMEM((8, nodes), F32),
            pltpu.VMEM((narrow - 1, 8, nodes), F32),
            dma((8,)),
            dma((wide,)),
            dma((wide,)),
            dma((wide - 1,)),
            dma((wide - 1,)),
            dma((narrow, chunks)),
            dma((narrow, chunks)),
            dma((narrow, chunks)),
            dma((wide // 2 - 1, chunks)),
            dma((wide // 2, chunks)),
            dma((wide // 2, 2, chunks)),
            dma((narrow - 1,)),
            dma((narrow - 1,)),
        ],
        compiler_params=pltpu.CompilerParams(
            collective_id=0, has_side_effects=True, vmem_limit_bytes=VMEM_LIMIT
        ),
        name="layers",
    )(
        send_blocks,
        tile_rows,
        tile_cols,
        tile_count,
        features,
        neighbor_first,
        self_first,
        self_second,
        neighbor_second,
        adjacency,
    )


def solution(mesh):
    in_specs = (
        P(("groups", "wide"), None),
        P(None, "narrow"),
        P(None, "narrow"),
        P(None, "narrow"),
        P(None, "narrow"),
        P(("groups", "wide"), None, None),
        P(("groups", "wide")),
        P(("groups", "wide")),
        P(("groups", "wide")),
        P(("groups", "wide"), None),
    )
    out_specs = P(("groups", "wide"), "narrow")
    body = functools.partial(shards, mesh.shape["wide"], mesh.shape["narrow"])
    return jax.shard_map(body, mesh=mesh, in_specs=in_specs, out_specs=out_specs, check_vma=False)
```

```python
import functools
import math

import jax
import jax.numpy as jnp
from jax import lax
from jax.experimental import pallas as pl
from jax.experimental.pallas import tpu as pltpu
from jax.sharding import PartitionSpec as P

EPSILON = 1e-06
MESH = pl.DeviceIdType.MESH
F32 = jnp.float32
BF16 = jnp.bfloat16
VMEM_LIMIT = 56 * 1024 * 1024


def dot(a, b):
    return jnp.dot(a, b, preferred_element_type=F32)


def main_kernel(
    wide,
    narrow,
    step,
    factor,
    sb_ref,
    rows_ref,
    cols_ref,
    count_ref,
    feat_hbm,
    n1_hbm,
    s1_hbm,
    s2_hbm,
    n2_hbm,
    adj_hbm,
    out_ref,
    feat_ref,
    n1_ref,
    tiles,
    a,
    inv,
    s1,
    s2,
    n2,
    own1,
    halo1,
    out1,
    every,
    halo2,
    table,
    table_in,
    sbv_ref,
    sbv_in,
    sb_in,
    pre,
    agg,
    hid,
    squares,
    part_sum,
    sums,
    load_sem,
    sb_send,
    sb_recv,
    halo_send,
    halo_recv,
    right_send,
    left_send,
    hid_recv,
    across_send,
    peer_send,
    every_recv,
    sum_send,
    sum_recv,
):
    num_blocks, blk, cols = own1.shape
    nodes = num_blocks * blk
    slots = sb_ref.shape[1]
    depth = slots * blk
    chunks = nodes // step
    per = step // blk
    pairs = wide // 2
    width = a.shape[1]
    num_tiles = rows_ref.shape[0]
    me = lax.axis_index("wide")
    n = lax.axis_index("narrow")
    pair = me // 2
    core = lax.rem(me, 2)
    other = 1 - core

    sources = [feat_hbm, n1_hbm, adj_hbm, s1_hbm, n2_hbm, s2_hbm]
    targets = [feat_ref, n1_ref, tiles.at[pl.ds(0, num_tiles)], s1, n2, s2]
    loads = [
        pltpu.make_async_copy(src, dst, load_sem.at[i])
        for i, (src, dst) in enumerate(zip(sources, targets))
    ]
    for load in loads:
        load.start()

    barrier = pltpu.get_barrier_semaphore()
    for d in range(1, wide):
        pl.semaphore_signal(
            barrier, inc=1, device_id={"wide": lax.rem(me + d, wide)}, device_id_type=MESH
        )
    for d in range(1, narrow):
        pl.semaphore_signal(
            barrier, inc=1, device_id={"narrow": lax.rem(n + d, narrow)}, device_id_type=MESH
        )

    lane = lax.broadcasted_iota(jnp.int32, (8, 128), 1)
    for q in range(wide):
        value = jnp.zeros((8, 128), jnp.int32)
        for s in range(slots):
            value = jnp.where(lane == s, sb_ref[q, s], value)
        sbv_ref[q] = value

    loads[0].wait()
    loads[1].wait()

    def rows_of(c):
        return pl.ds(pl.multiple_of(c * step, step), step)

    @pl.loop(0, num_blocks // 4)
    def _(b):
        at = pl.ds(pl.multiple_of(b * (4 * blk), blk), 4 * blk)
        own1[pl.ds(b * 4, 4)] = dot(feat_ref[at, :], n1_ref[...]).astype(BF16).reshape(4, blk, cols)

    pl.semaphore_wait(barrier, wide + narrow - 2)

    far = wide // 2
    order = [far] + [d for d in range(1, wide) if d != far]

    def sb_copy(q, p):
        return pltpu.make_async_remote_copy(
            src_ref=sbv_ref.at[q],
            dst_ref=sbv_in.at[p],
            send_sem=sb_send.at[q],
            recv_sem=sb_recv.at[p],
            device_id={"wide": q},
            device_id_type=MESH,
        )

    def halo_copy(d):
        return pltpu.make_async_remote_copy(
            src_ref=out1.at[d - 1],
            dst_ref=halo1.at[d - 1],
            send_sem=halo_send.at[d - 1],
            recv_sem=halo_recv.at[d - 1],
            device_id={"wide": lax.rem(me + d, wide)},
            device_id_type=MESH,
        )

    def halo_term(d, c):
        p = lax.rem(me + wide - d, wide)
        at = pl.ds(pl.multiple_of(nodes + p * depth, blk), depth)
        return dot(a[rows_of(c), at], halo1[d - 1])

    def hid_copy(o, c, sems, target):
        return pltpu.make_async_remote_copy(
            src_ref=hid.at[o, rows_of(c)],
            dst_ref=hid.at[o, rows_of(c)],
            send_sem=sems.at[o, c],
            recv_sem=hid_recv.at[o, c],
            device_id={"narrow": target},
            device_id_type=MESH,
        )

    def to_right(o, c):
        return hid_copy(o, c, right_send, lax.rem(n + 1, narrow))

    def to_left(o, c):
        return hid_copy(o, c, left_send, lax.rem(n + narrow - 1, narrow))

    def blocks_of(c):
        return pl.ds(c * per, per)

    def across_copy(dx, c):
        return pltpu.make_async_remote_copy(
            src_ref=every.at[0, core, blocks_of(c)],
            dst_ref=every.at[dx, core, blocks_of(c)],
            send_sem=across_send.at[dx - 1, c],
            recv_sem=every_recv.at[dx, core, c],
            device_id={"wide": lax.rem(pair + dx, pairs) * 2 + core},
            device_id_type=MESH,
        )

    def peer_copy(dx, side, c):
        return pltpu.make_async_remote_copy(
            src_ref=every.at[dx, side, blocks_of(c)],
            dst_ref=every.at[dx, side, blocks_of(c)],
            send_sem=peer_send.at[dx, c],
            recv_sem=every_recv.at[dx, side, c],
            device_id={"wide": pair * 2 + other},
            device_id_type=MESH,
        )

    def pass_on(c):
        for dx in range(1, pairs):
            across_copy(dx, c).wait_recv()
            peer_copy(dx, core, c).start()

    for d in order:
        q = lax.rem(me + d, wide)
        for s in range(slots):
            out1[d - 1, s * blk : (s + 1) * blk, :] = own1[sb_ref[q, s]]
        halo_copy(d).start()
    for d in order:
        sb_copy(lax.rem(me + d, wide), me).start()
    sbv_in[me] = sbv_ref[me]

    block_row = lax.broadcasted_iota(jnp.int32, (num_blocks, 128), 0)
    block_col = lax.broadcasted_iota(jnp.int32, (num_blocks, 128), 1)
    live = count_ref[0]

    def key_of(t):
        return jnp.where(t < live, rows_ref[t] * 128 + cols_ref[t], -1 - t)

    def gather_keys(t, keys):
        return jnp.where(lane == t, key_of(t), keys)

    keys = lax.fori_loop(0, num_tiles, gather_keys, jnp.full((8, 128), -1000, jnp.int32))

    def link(t, state):
        last, prev = state
        key = key_of(t)
        last = jnp.where(block_row * 128 + block_col == key, t, last)
        prev = jnp.where((keys == key) & (lane > t), t, prev)
        return last, prev

    empty = (
        jnp.full((num_blocks, 128), num_tiles, jnp.int32),
        jnp.full((8, 128), num_tiles, jnp.int32),
    )
    last, prev = lax.fori_loop(0, num_tiles, link, empty)
    table[0:num_blocks, :] = last
    table[num_blocks : num_blocks + 8, :] = prev
    to_scalar = pltpu.make_async_copy(table, table_in, load_sem.at[7])
    to_scalar.start()
    to_scalar.wait()

    loads[2].wait()
    tiles[num_tiles] = jnp.zeros((blk, blk), BF16)

    @pl.loop(0, num_tiles)
    def _(t):
        tiles[t] += tiles[table_in[num_blocks, t]]

    @pl.loop(0, num_blocks)
    def _(b):
        for j in range(width // blk):
            at = pl.ds(pl.multiple_of(b * blk, blk), blk)
            a[at, j * blk : (j + 1) * blk] = tiles[table_in[b, j]]

    loads[3].wait()
    ones_tall = jnp.ones((width, blk), BF16)

    @pl.loop(0, chunks)
    def _(c):
        pre[rows_of(c), :] = dot(feat_ref[rows_of(c), :], s1[...])
        inv[rows_of(c), :] = 1.0 / jnp.maximum(dot(a[rows_of(c), :], ones_tall), 1.0)
        agg[rows_of(c), :] = dot(a[rows_of(c), 0:nodes], own1[...].reshape(nodes, cols))

    for d in order[1:] + order[:1]:
        halo_copy(d).wait_recv()
        if d != order[0]:

            @pl.loop(0, chunks)
            def _(c):
                agg[rows_of(c), :] += halo_term(d, c)

    @pl.loop(0, chunks)
    def _(c):
        mean = (agg[rows_of(c), :] + halo_term(order[0], c)) * inv[rows_of(c), 0:1]
        hid[n, rows_of(c)] = jnp.maximum(pre[rows_of(c), :] + mean, 0.0).astype(BF16)

        @pl.when(n < narrow - 1)
        def _():
            to_right(n, c).start()

        @pl.when(n > 0)
        def _():
            to_left(n, c).start()

    for d in order:
        sb_copy(me, lax.rem(me + d, wide)).wait_recv()
    to_scalar = pltpu.make_async_copy(sbv_in, sb_in, load_sem.at[6])
    to_scalar.start()
    to_scalar.wait()
    loads[4].wait()
    loads[5].wait()

    def consume(o, c, first=False):
        h = hid[o, rows_of(c)]
        at = pl.ds(pl.multiple_of(o * cols, cols), cols)
        wide_h = h.astype(F32)
        square = jnp.sum(wide_h * wide_h, axis=1, keepdims=True)
        self_term = dot(h, s2[at, :])
        neighbor_term = dot(h, n2[at, :])
        if first:
            squares[rows_of(c), :] = jnp.broadcast_to(square, (step, squares.shape[1]))
            pre[rows_of(c), :] = self_term
            agg[rows_of(c), :] = neighbor_term
        else:
            squares[rows_of(c), :] += square
            pre[rows_of(c), :] += self_term
            agg[rows_of(c), :] += neighbor_term

    @pl.loop(0, chunks)
    def _(c):
        consume(n, c, first=True)

    def finish(c):
        scale = lax.rsqrt(squares[rows_of(c), 0:1] + EPSILON)
        pre[rows_of(c), :] = pre[rows_of(c), :] * scale
        projected = (agg[rows_of(c), :] * scale).astype(BF16)
        every[0, core, blocks_of(c)] = projected.reshape(per, blk, cols)
        for dx in range(1, pairs):
            across_copy(dx, c).start()
        peer_copy(0, core, c).start()

    longest = jnp.maximum(n, narrow - 1 - n)

    @pl.loop(1, narrow)
    def _(dist):
        @pl.loop(0, chunks)
        def _(c):
            @pl.when(n >= dist)
            def _():
                to_right(n - dist, c).wait_recv()

                @pl.when(n < narrow - 1)
                def _():
                    to_right(n - dist, c).start()

            @pl.when(n + dist < narrow)
            def _():
                to_left(n + dist, c).wait_recv()

                @pl.when(n > 0)
                def _():
                    to_left(n + dist, c).start()

            @pl.when(n >= dist)
            def _():
                consume(n - dist, c)

            @pl.when(n + dist < narrow)
            def _():
                consume(n + dist, c)

            @pl.when(dist == longest)
            def _():
                finish(c)

                @pl.when(c > 1)
                def _():
                    pass_on(c - 2)

    @pl.loop(0, chunks)
    def _(c):
        agg[rows_of(c), :] = dot(a[rows_of(c), 0:nodes], every[0, core].reshape(nodes, cols))

    pass_on(chunks - 2)
    pass_on(chunks - 1)
    for dx in range(pairs):
        for c in range(chunks):
            peer_copy(dx, other, c).wait_recv()

    for p in range(wide):
        dx = lax.rem(pair + pairs - p // 2, pairs)
        for s in range(slots):
            at = p * depth + s * blk
            halo2[at : at + blk, :] = every[dx, p % 2, sb_in[p, 0, s]]

    value = pre[...] + (agg[...] + dot(a[:, nodes:width], halo2[...])) * inv[:, 0:1]
    pre[...] = value
    row_sum = jnp.sum(value * value, axis=1, keepdims=True)
    part_sum[...] = jnp.broadcast_to(row_sum, (nodes, blk)).T[0:8, :]

    def sum_copy(d):
        return pltpu.make_async_remote_copy(
            src_ref=part_sum,
            dst_ref=sums.at[d - 1],
            send_sem=sum_send.at[d - 1],
            recv_sem=sum_recv.at[d - 1],
            device_id={"narrow": lax.rem(n + d, narrow)},
            device_id_type=MESH,
        )

    for d in range(1, narrow):
        sum_copy(d).start()
    for d in range(1, narrow):
        sum_copy(d).wait_recv()

    @pl.loop(0, chunks)
    def _(c):
        summed = part_sum[:, rows_of(c)]
        for d in range(1, narrow):
            summed = summed + sums[d - 1, :, rows_of(c)]
        scale = lax.rsqrt(summed + EPSILON) * factor
        turned = jnp.broadcast_to(scale[0:1, :], (blk, step)).T
        out_ref[rows_of(c), :] = (pre[rows_of(c), :] * turned[:, 0:1]).astype(BF16)

    for d in range(1, narrow):
        sum_copy(d).wait_send()
    for d in order:
        halo_copy(d).wait_send()
        sb_copy(lax.rem(me + d, wide), me).wait_send()

    @pl.loop(0, chunks)
    def _(c):
        for dx in range(1, pairs):
            across_copy(dx, c).wait_send()
            peer_copy(dx, core, c).wait_send()
        peer_copy(0, core, c).wait_send()

    @pl.loop(0, narrow)
    def _(dist):
        @pl.loop(0, chunks)
        def _(c):
            @pl.when((n >= dist) & (n < narrow - 1))
            def _():
                to_right(n - dist, c).wait_send()

            @pl.when((n + dist < narrow) & (n > 0))
            def _():
                to_left(n + dist, c).wait_send()


def shards(
    wide,
    narrow,
    features,
    self_first,
    neighbor_first,
    self_second,
    neighbor_second,
    adjacency,
    tile_rows,
    tile_cols,
    tile_count,
    send_blocks,
):
    blk = adjacency.shape[1]
    nodes, in_width = features.shape
    num_blocks = nodes // blk
    slots = send_blocks.shape[1]
    hidden_width, cols = self_second.shape
    width = nodes + wide * slots * blk
    step = 2 * blk
    chunks = nodes // step
    vmem = pl.BlockSpec(memory_space=pltpu.VMEM)
    smem = pl.BlockSpec(memory_space=pltpu.SMEM)
    anywhere = pl.BlockSpec(memory_space=pl.ANY)
    num_tiles = adjacency.shape[0]
    depth = slots * blk
    dma = pltpu.SemaphoreType.DMA
    return pl.pallas_call(
        functools.partial(main_kernel, wide, narrow, step, math.sqrt(hidden_width)),
        out_shape=jax.ShapeDtypeStruct((nodes, cols), BF16),
        in_specs=[smem] * 4 + [anywhere] * 6,
        out_specs=vmem,
        scratch_shapes=[
            pltpu.VMEM((nodes, in_width), BF16),
            pltpu.VMEM((in_width, cols), BF16),
            pltpu.VMEM((num_tiles + 1, blk, blk), BF16),
            pltpu.VMEM((nodes, width), BF16),
            pltpu.VMEM((nodes, blk), F32),
            pltpu.VMEM((in_width, cols), BF16),
            pltpu.VMEM((hidden_width, cols), BF16),
            pltpu.VMEM((hidden_width, cols), BF16),
            pltpu.VMEM((num_blocks, blk, cols), BF16),
            pltpu.VMEM((wide - 1, depth, cols), BF16),
            pltpu.VMEM((wide - 1, depth, cols), BF16),
            pltpu.VMEM((wide // 2, 2, num_blocks, blk, cols), BF16),
            pltpu.VMEM((wide * depth, cols), BF16),
            pltpu.VMEM((num_blocks + 8, 128), jnp.int32),
            pltpu.SMEM((num_blocks + 8, 128), jnp.int32),
            pltpu.VMEM((wide, 8, 128), jnp.int32),
            pltpu.VMEM((wide, 8, 128), jnp.int32),
            pltpu.SMEM((wide, 8, 128), jnp.int32),
            pltpu.VMEM((nodes, cols), F32),
            pltpu.VMEM((nodes, cols), F32),
            pltpu.VMEM((narrow, nodes, cols), BF16),
            pltpu.VMEM((nodes, 128), F32),
            pltpu.VMEM((8, nodes), F32),
            pltpu.VMEM((narrow - 1, 8, nodes), F32),
            dma((8,)),
            dma((wide,)),
            dma((wide,)),
            dma((wide - 1,)),
            dma((wide - 1,)),
            dma((narrow, chunks)),
            dma((narrow, chunks)),
            dma((narrow, chunks)),
            dma((wide // 2 - 1, chunks)),
            dma((wide // 2, chunks)),
            dma((wide // 2, 2, chunks)),
            dma((narrow - 1,)),
            dma((narrow - 1,)),
        ],
        compiler_params=pltpu.CompilerParams(
            collective_id=0, has_side_effects=True, vmem_limit_bytes=VMEM_LIMIT
        ),
        name="layers",
    )(
        send_blocks,
        tile_rows,
        tile_cols,
        tile_count,
        features,
        neighbor_first,
        self_first,
        self_second,
        neighbor_second,
        adjacency,
    )


def solution(mesh):
    in_specs = (
        P(("groups", "wide"), None),
        P(None, "narrow"),
        P(None, "narrow"),
        P(None, "narrow"),
        P(None, "narrow"),
        P(("groups", "wide"), None, None),
        P(("groups", "wide")),
        P(("groups", "wide")),
        P(("groups", "wide")),
        P(("groups", "wide"), None),
    )
    out_specs = P(("groups", "wide"), "narrow")
    body = functools.partial(shards, mesh.shape["wide"], mesh.shape["narrow"])
    return jax.shard_map(body, mesh=mesh, in_specs=in_specs, out_specs=out_specs, check_vma=False)
```

```python
import functools
import math

import jax
import jax.numpy as jnp
from jax import lax
from jax.experimental import pallas as pl
from jax.experimental.pallas import tpu as pltpu
from jax.sharding import PartitionSpec as P

EPSILON = 1e-06
MESH = pl.DeviceIdType.MESH
F32 = jnp.float32
BF16 = jnp.bfloat16
VMEM_LIMIT = 56 * 1024 * 1024


def dot(a, b):
    return jnp.dot(a, b, preferred_element_type=F32)


def main_kernel(
    wide,
    narrow,
    step,
    factor,
    sb_ref,
    rows_ref,
    cols_ref,
    count_ref,
    feat_hbm,
    n1_hbm,
    s1_hbm,
    s2_hbm,
    n2_hbm,
    adj_hbm,
    out_ref,
    feat_ref,
    n1_ref,
    tiles,
    a,
    inv,
    s1,
    s2,
    n2,
    own1,
    halo1,
    out1,
    every,
    halo2,
    table,
    table_in,
    sbv_ref,
    sbv_in,
    sb_in,
    pre,
    agg,
    hid,
    squares,
    part_sum,
    sums,
    load_sem,
    sb_send,
    sb_recv,
    halo_send,
    halo_recv,
    right_send,
    left_send,
    hid_recv,
    across_send,
    peer_send,
    every_recv,
    sum_send,
    sum_recv,
):
    num_blocks, blk, cols = own1.shape
    nodes = num_blocks * blk
    slots = sb_ref.shape[1]
    depth = slots * blk
    chunks = nodes // step
    per = step // blk
    pairs = wide // 2
    width = a.shape[1]
    num_tiles = rows_ref.shape[0]
    me = lax.axis_index("wide")
    n = lax.axis_index("narrow")
    pair = me // 2
    core = lax.rem(me, 2)
    other = 1 - core

    sources = [feat_hbm, n1_hbm, adj_hbm, s1_hbm, n2_hbm, s2_hbm]
    targets = [feat_ref, n1_ref, tiles.at[pl.ds(0, num_tiles)], s1, n2, s2]
    loads = [
        pltpu.make_async_copy(src, dst, load_sem.at[i])
        for i, (src, dst) in enumerate(zip(sources, targets))
    ]
    for load in loads:
        load.start()

    barrier = pltpu.get_barrier_semaphore()
    for d in range(1, wide):
        pl.semaphore_signal(
            barrier, inc=1, device_id={"wide": lax.rem(me + d, wide)}, device_id_type=MESH
        )
    for d in range(1, narrow):
        pl.semaphore_signal(
            barrier, inc=1, device_id={"narrow": lax.rem(n + d, narrow)}, device_id_type=MESH
        )

    lane = lax.broadcasted_iota(jnp.int32, (8, 128), 1)
    for q in range(wide):
        value = jnp.zeros((8, 128), jnp.int32)
        for s in range(slots):
            value = jnp.where(lane == s, sb_ref[q, s], value)
        sbv_ref[q] = value

    loads[0].wait()
    loads[1].wait()

    def rows_of(c):
        return pl.ds(pl.multiple_of(c * step, step), step)

    @pl.loop(0, num_blocks // 4)
    def _(b):
        at = pl.ds(pl.multiple_of(b * (4 * blk), blk), 4 * blk)
        own1[pl.ds(b * 4, 4)] = dot(feat_ref[at, :], n1_ref[...]).astype(BF16).reshape(4, blk, cols)

    pl.semaphore_wait(barrier, wide + narrow - 2)

    far = wide // 2
    order = [far] + [d for d in range(1, wide) if d != far]

    def sb_copy(q, p):
        return pltpu.make_async_remote_copy(
            src_ref=sbv_ref.at[q],
            dst_ref=sbv_in.at[p],
            send_sem=sb_send.at[q],
            recv_sem=sb_recv.at[p],
            device_id={"wide": q},
            device_id_type=MESH,
        )

    def halo_copy(d):
        return pltpu.make_async_remote_copy(
            src_ref=out1.at[d - 1],
            dst_ref=halo1.at[d - 1],
            send_sem=halo_send.at[d - 1],
            recv_sem=halo_recv.at[d - 1],
            device_id={"wide": lax.rem(me + d, wide)},
            device_id_type=MESH,
        )

    def halo_term(d, c):
        p = lax.rem(me + wide - d, wide)
        at = pl.ds(pl.multiple_of(nodes + p * depth, blk), depth)
        return dot(a[rows_of(c), at], halo1[d - 1])

    def hid_copy(o, c, sems, target):
        return pltpu.make_async_remote_copy(
            src_ref=hid.at[o, rows_of(c)],
            dst_ref=hid.at[o, rows_of(c)],
            send_sem=sems.at[o, c],
            recv_sem=hid_recv.at[o, c],
            device_id={"narrow": target},
            device_id_type=MESH,
        )

    def to_right(o, c):
        return hid_copy(o, c, right_send, lax.rem(n + 1, narrow))

    def to_left(o, c):
        return hid_copy(o, c, left_send, lax.rem(n + narrow - 1, narrow))

    def blocks_of(c):
        return pl.ds(c * per, per)

    def across_copy(dx, c):
        return pltpu.make_async_remote_copy(
            src_ref=every.at[0, core, blocks_of(c)],
            dst_ref=every.at[dx, core, blocks_of(c)],
            send_sem=across_send.at[dx - 1, c],
            recv_sem=every_recv.at[dx, core, c],
            device_id={"wide": lax.rem(pair + dx, pairs) * 2 + core},
            device_id_type=MESH,
        )

    def peer_copy(dx, side, c):
        return pltpu.make_async_remote_copy(
            src_ref=every.at[dx, side, blocks_of(c)],
            dst_ref=every.at[dx, side, blocks_of(c)],
            send_sem=peer_send.at[dx, c],
            recv_sem=every_recv.at[dx, side, c],
            device_id={"wide": pair * 2 + other},
            device_id_type=MESH,
        )

    def pass_on(c):
        for dx in range(1, pairs):
            across_copy(dx, c).wait_recv()
            peer_copy(dx, core, c).start()

    for d in order:
        q = lax.rem(me + d, wide)
        for s in range(slots):
            out1[d - 1, s * blk : (s + 1) * blk, :] = own1[sb_ref[q, s]]
        halo_copy(d).start()
    for d in order:
        sb_copy(lax.rem(me + d, wide), me).start()
    sbv_in[me] = sbv_ref[me]

    block_row = lax.broadcasted_iota(jnp.int32, (num_blocks, 128), 0)
    block_col = lax.broadcasted_iota(jnp.int32, (num_blocks, 128), 1)
    live = count_ref[0]

    def key_of(t):
        return jnp.where(t < live, rows_ref[t] * 128 + cols_ref[t], -1 - t)

    def gather_keys(t, keys):
        return jnp.where(lane == t, key_of(t), keys)

    keys = lax.fori_loop(0, num_tiles, gather_keys, jnp.full((8, 128), -1000, jnp.int32))

    def link(t, state):
        last, prev = state
        key = key_of(t)
        last = jnp.where(block_row * 128 + block_col == key, t, last)
        prev = jnp.where((keys == key) & (lane > t), t, prev)
        return last, prev

    empty = (
        jnp.full((num_blocks, 128), num_tiles, jnp.int32),
        jnp.full((8, 128), num_tiles, jnp.int32),
    )
    last, prev = lax.fori_loop(0, num_tiles, link, empty)
    table[0:num_blocks, :] = last
    table[num_blocks : num_blocks + 8, :] = prev
    to_scalar = pltpu.make_async_copy(table, table_in, load_sem.at[7])
    to_scalar.start()
    to_scalar.wait()

    loads[2].wait()
    tiles[num_tiles] = jnp.zeros((blk, blk), BF16)

    @pl.loop(0, num_tiles)
    def _(t):
        tiles[t] += tiles[table_in[num_blocks, t]]

    @pl.loop(0, num_blocks)
    def _(b):
        for j in range(width // blk):
            at = pl.ds(pl.multiple_of(b * blk, blk), blk)
            a[at, j * blk : (j + 1) * blk] = tiles[table_in[b, j]]

    loads[3].wait()
    ones_tall = jnp.ones((width, blk), BF16)

    @pl.loop(0, chunks)
    def _(c):
        pre[rows_of(c), :] = dot(feat_ref[rows_of(c), :], s1[...])
        inv[rows_of(c), :] = 1.0 / jnp.maximum(dot(a[rows_of(c), :], ones_tall), 1.0)
        agg[rows_of(c), :] = dot(a[rows_of(c), 0:nodes], own1[...].reshape(nodes, cols))

    for d in order[1:] + order[:1]:
        halo_copy(d).wait_recv()
        if d != order[0]:

            @pl.loop(0, chunks)
            def _(c):
                agg[rows_of(c), :] += halo_term(d, c)

    @pl.loop(0, chunks)
    def _(c):
        mean = (agg[rows_of(c), :] + halo_term(order[0], c)) * inv[rows_of(c), 0:1]
        hid[n, rows_of(c)] = jnp.maximum(pre[rows_of(c), :] + mean, 0.0).astype(BF16)

        @pl.when(n < narrow - 1)
        def _():
            to_right(n, c).start()

        @pl.when(n > 0)
        def _():
            to_left(n, c).start()

    for d in order:
        sb_copy(me, lax.rem(me + d, wide)).wait_recv()
    to_scalar = pltpu.make_async_copy(sbv_in, sb_in, load_sem.at[6])
    to_scalar.start()
    to_scalar.wait()
    loads[4].wait()
    loads[5].wait()

    def consume(o, c, first=False):
        h = hid[o, rows_of(c)]
        at = pl.ds(pl.multiple_of(o * cols, cols), cols)
        wide_h = h.astype(F32)
        square = jnp.sum(wide_h * wide_h, axis=1, keepdims=True)
        self_term = dot(h, s2[at, :])
        neighbor_term = dot(h, n2[at, :])
        if first:
            squares[rows_of(c), :] = jnp.broadcast_to(square, (step, squares.shape[1]))
            pre[rows_of(c), :] = self_term
            agg[rows_of(c), :] = neighbor_term
        else:
            squares[rows_of(c), :] += square
            pre[rows_of(c), :] += self_term
            agg[rows_of(c), :] += neighbor_term

    @pl.loop(0, chunks)
    def _(c):
        consume(n, c, first=True)

    def finish(c):
        scale = lax.rsqrt(squares[rows_of(c), 0:1] + EPSILON)
        pre[rows_of(c), :] = pre[rows_of(c), :] * scale
        projected = (agg[rows_of(c), :] * scale).astype(BF16)
        every[0, core, blocks_of(c)] = projected.reshape(per, blk, cols)
        for dx in range(1, pairs):
            across_copy(dx, c).start()
        peer_copy(0, core, c).start()

    longest = jnp.maximum(n, narrow - 1 - n)

    @pl.loop(1, narrow)
    def _(dist):
        @pl.loop(0, chunks)
        def _(c):
            @pl.when(n >= dist)
            def _():
                to_right(n - dist, c).wait_recv()

                @pl.when(n < narrow - 1)
                def _():
                    to_right(n - dist, c).start()

            @pl.when(n + dist < narrow)
            def _():
                to_left(n + dist, c).wait_recv()

                @pl.when(n > 0)
                def _():
                    to_left(n + dist, c).start()

            @pl.when(n >= dist)
            def _():
                consume(n - dist, c)

            @pl.when(n + dist < narrow)
            def _():
                consume(n + dist, c)

            @pl.when(dist == longest)
            def _():
                finish(c)

                @pl.when(c > 1)
                def _():
                    pass_on(c - 2)

    pass_on(chunks - 2)
    agg[...] = dot(a[:, 0:nodes], every[0, core].reshape(nodes, cols))

    pass_on(chunks - 1)
    for dx in range(pairs):
        for c in range(chunks):
            peer_copy(dx, other, c).wait_recv()

    for p in range(wide):
        dx = lax.rem(pair + pairs - p // 2, pairs)
        for s in range(slots):
            at = p * depth + s * blk
            halo2[at : at + blk, :] = every[dx, p % 2, sb_in[p, 0, s]]

    value = pre[...] + (agg[...] + dot(a[:, nodes:width], halo2[...])) * inv[:, 0:1]
    pre[...] = value
    row_sum = jnp.sum(value * value, axis=1, keepdims=True)
    part_sum[...] = jnp.broadcast_to(row_sum, (nodes, blk)).T[0:8, :]

    def sum_copy(d):
        return pltpu.make_async_remote_copy(
            src_ref=part_sum,
            dst_ref=sums.at[d - 1],
            send_sem=sum_send.at[d - 1],
            recv_sem=sum_recv.at[d - 1],
            device_id={"narrow": lax.rem(n + d, narrow)},
            device_id_type=MESH,
        )

    for d in range(1, narrow):
        sum_copy(d).start()
    for d in range(1, narrow):
        sum_copy(d).wait_recv()

    @pl.loop(0, chunks)
    def _(c):
        summed = part_sum[:, rows_of(c)]
        for d in range(1, narrow):
            summed = summed + sums[d - 1, :, rows_of(c)]
        scale = lax.rsqrt(summed + EPSILON) * factor
        turned = jnp.broadcast_to(scale[0:1, :], (blk, step)).T
        out_ref[rows_of(c), :] = (pre[rows_of(c), :] * turned[:, 0:1]).astype(BF16)

    for d in range(1, narrow):
        sum_copy(d).wait_send()
    for d in order:
        halo_copy(d).wait_send()
        sb_copy(lax.rem(me + d, wide), me).wait_send()

    @pl.loop(0, chunks)
    def _(c):
        for dx in range(1, pairs):
            across_copy(dx, c).wait_send()
            peer_copy(dx, core, c).wait_send()
        peer_copy(0, core, c).wait_send()

    @pl.loop(0, narrow)
    def _(dist):
        @pl.loop(0, chunks)
        def _(c):
            @pl.when((n >= dist) & (n < narrow - 1))
            def _():
                to_right(n - dist, c).wait_send()

            @pl.when((n + dist < narrow) & (n > 0))
            def _():
                to_left(n + dist, c).wait_send()


def shards(
    wide,
    narrow,
    features,
    self_first,
    neighbor_first,
    self_second,
    neighbor_second,
    adjacency,
    tile_rows,
    tile_cols,
    tile_count,
    send_blocks,
):
    blk = adjacency.shape[1]
    nodes, in_width = features.shape
    num_blocks = nodes // blk
    slots = send_blocks.shape[1]
    hidden_width, cols = self_second.shape
    width = nodes + wide * slots * blk
    step = 2 * blk
    chunks = nodes // step
    vmem = pl.BlockSpec(memory_space=pltpu.VMEM)
    smem = pl.BlockSpec(memory_space=pltpu.SMEM)
    anywhere = pl.BlockSpec(memory_space=pl.ANY)
    num_tiles = adjacency.shape[0]
    depth = slots * blk
    dma = pltpu.SemaphoreType.DMA
    return pl.pallas_call(
        functools.partial(main_kernel, wide, narrow, step, math.sqrt(hidden_width)),
        out_shape=jax.ShapeDtypeStruct((nodes, cols), BF16),
        in_specs=[smem] * 4 + [anywhere] * 6,
        out_specs=vmem,
        scratch_shapes=[
            pltpu.VMEM((nodes, in_width), BF16),
            pltpu.VMEM((in_width, cols), BF16),
            pltpu.VMEM((num_tiles + 1, blk, blk), BF16),
            pltpu.VMEM((nodes, width), BF16),
            pltpu.VMEM((nodes, blk), F32),
            pltpu.VMEM((in_width, cols), BF16),
            pltpu.VMEM((hidden_width, cols), BF16),
            pltpu.VMEM((hidden_width, cols), BF16),
            pltpu.VMEM((num_blocks, blk, cols), BF16),
            pltpu.VMEM((wide - 1, depth, cols), BF16),
            pltpu.VMEM((wide - 1, depth, cols), BF16),
            pltpu.VMEM((wide // 2, 2, num_blocks, blk, cols), BF16),
            pltpu.VMEM((wide * depth, cols), BF16),
            pltpu.VMEM((num_blocks + 8, 128), jnp.int32),
            pltpu.SMEM((num_blocks + 8, 128), jnp.int32),
            pltpu.VMEM((wide, 8, 128), jnp.int32),
            pltpu.VMEM((wide, 8, 128), jnp.int32),
            pltpu.SMEM((wide, 8, 128), jnp.int32),
            pltpu.VMEM((nodes, cols), F32),
            pltpu.VMEM((nodes, cols), F32),
            pltpu.VMEM((narrow, nodes, cols), BF16),
            pltpu.VMEM((nodes, 128), F32),
            pltpu.VMEM((8, nodes), F32),
            pltpu.VMEM((narrow - 1, 8, nodes), F32),
            dma((8,)),
            dma((wide,)),
            dma((wide,)),
            dma((wide - 1,)),
            dma((wide - 1,)),
            dma((narrow, chunks)),
            dma((narrow, chunks)),
            dma((narrow, chunks)),
            dma((wide // 2 - 1, chunks)),
            dma((wide // 2, chunks)),
            dma((wide // 2, 2, chunks)),
            dma((narrow - 1,)),
            dma((narrow - 1,)),
        ],
        compiler_params=pltpu.CompilerParams(
            collective_id=0, has_side_effects=True, vmem_limit_bytes=VMEM_LIMIT
        ),
        name="layers",
    )(
        send_blocks,
        tile_rows,
        tile_cols,
        tile_count,
        features,
        neighbor_first,
        self_first,
        self_second,
        neighbor_second,
        adjacency,
    )


def solution(mesh):
    in_specs = (
        P(("groups", "wide"), None),
        P(None, "narrow"),
        P(None, "narrow"),
        P(None, "narrow"),
        P(None, "narrow"),
        P(("groups", "wide"), None, None),
        P(("groups", "wide")),
        P(("groups", "wide")),
        P(("groups", "wide")),
        P(("groups", "wide"), None),
    )
    out_specs = P(("groups", "wide"), "narrow")
    body = functools.partial(shards, mesh.shape["wide"], mesh.shape["narrow"])
    return jax.shard_map(body, mesh=mesh, in_specs=in_specs, out_specs=out_specs, check_vma=False)
```
